256 devices in a mesh: ctx: 16 (over y, x_lo, core), head: 16 (over z, x_hi).
Axes of the slice: x: 4 (x_hi: 2, x_lo: 2; x = x_hi * 2 + x_lo), y: 4, z: 8, core: 2. Of those that a mesh axis runs over, the one named last changes fastest.
Arguments:
- query: bfloat16 [4096, 4096], P('ctx', 'head'), may hold values from -120 to 120
- keys: bfloat16 [4096, 4096], P('ctx', 'head'), may hold values from -9 to 9
- values: bfloat16 [4096, 4096], P('ctx', 'head'), may hold values from -6 to 6
- out_grad: bfloat16 [4096, 4096], P('ctx', 'head'), may hold values from -0.625 to 0.625
- gate_left: bfloat16 [4096, 512], P('head'), may hold values from -0.375 to 0.375
- up_left: bfloat16 [4096, 512], P('head'), may hold values from -0.375 to 0.375
- gate_right: bfloat16 [512, 11008], P(None, 'head'), may hold values from -0.25 to 0.25
- up_right: bfloat16 [512, 11008], P(None, 'head'), may hold values from -0.25 to 0.25
- down_left: bfloat16 [11008, 512], P('head'), may hold values from -0.25 to 0.25
- down_right: bfloat16 [512, 4096], P(None, 'head'), may hold values from -0.09375 to 0.09375
- block_order: int32 [32], replicated, may hold values from 0 to 31, each once
- doc_lengths: int32 [4], replicated, may hold values from 1 to 2048, 4096 in all
Outputs:
- grad_query: bfloat16 [4096, 4096], P('ctx', 'head')
- grad_keys: bfloat16 [4096, 4096], P('ctx', 'head')
- grad_values: bfloat16 [4096, 4096], P('ctx', 'head')
- grad_gate_left: float32 [4096, 512], P('head', 'ctx')
- grad_up_left: float32 [4096, 512], P('head', 'ctx')
- grad_down_left: float32 [11008, 512], P('head', 'ctx')
- grad_gate_right: float32 [512, 11008], P('ctx', 'head')
- grad_up_right: float32 [512, 11008], P('ctx', 'head')
- grad_down_right: float32 [512, 4096], P('ctx', 'head')
The draws below stay inside these ranges and needn't reach their ends.
All inputs are finite; a program needn't handle non-finite values.
Results may differ from the reference program's by a relative error of at most 0.038.
Values may be sent and summed in bfloat16 or wider, within the bound.
No kernel may reach another device: no remote copies, remote signals or barrier semaphores. Data moves between devices by JAX's collectives and lax.ppermute only.
A program may use at most 128 MiB of HBM per device.

```python
import math
import jax
import jax.numpy as jnp
import numpy as np
from jax import lax

D = 4096
HEADS = 32
HD = 128
FF = 11008
R = 512
TOK_DEV = 256
DOCS = 4
TOKENS = 4096
BLOCKS = 32


def base_keys(key):
    return 1.4 * jax.random.truncated_normal(key, -6.0, 6.0, (TOKENS, D), jnp.float32)


def draw_query(key, part):
    key = jax.random.fold_in(key, 5)
    drawn = 1.4 * jax.random.truncated_normal(key, -6.0, 6.0, (TOKENS, D), jnp.float32)
    return drawn.astype(jnp.bfloat16)


def draw_keys(key, part):
    common = base_keys(key)
    return common.astype(jnp.bfloat16)


def shard_levels(own_key, shape, shards, smallest, largest):
    gain, own = 1.0, jax.random.fold_in(own_key, 6)
    for dim, parts in shards:
        draws = jnp.exp(jax.random.uniform(jax.random.fold_in(own, dim), (parts,), jnp.float32, smallest / len(shards), largest / len(shards)))
        gain = gain * jnp.repeat(draws, shape[dim] // parts).reshape([-1 if axis == dim else 1 for axis in range(len(shape))])
    return gain


def length_profile(count, total, most, slope):
    loads = [(1 << 20) // math.isqrt(standing ** slope) + 1 for standing in range(2, count + 1)]
    rest, counts = total - most - (count - 1), [1] * (count - 1)
    while rest > 0:
        movable = [i for i in range(count - 1) if counts[i] < most]
        pool, budget = sum([loads[i] for i in movable]), rest
        for i in movable:
            extra = min(most - counts[i], max(1, budget * loads[i] // pool), rest)
            counts[i] = counts[i] + extra
            rest = rest - extra
    return np.array([most] + counts)


def ragged(stream_key, amount, total, most, slope):
    if amount == 2:
        one = jax.random.randint(stream_key, (), max(1, total - most), min(most, total - 1) + 1)
        return jnp.stack([one, total - one])
    tallies = jnp.asarray(length_profile(amount, total, most, slope), jnp.int32)
    twos = (amount - 1) // 2
    giver, taker = tallies[1:1 + 2 * twos:2], tallies[2:2 + 2 * twos:2]
    slack = jnp.minimum(giver - 1, most - taker)
    passed = jax.random.randint(jax.random.fold_in(stream_key, 1), (twos,), 0, 1 << 20) % (slack + 1)
    tallies = tallies.at[1:1 + 2 * twos:2].set(giver - passed).at[2:2 + 2 * twos:2].set(taker + passed)
    return tallies[jax.random.permutation(jax.random.fold_in(stream_key, 2), amount)]


def noise(rng, shape, width, most, shards=(), held_as=jnp.bfloat16):
    factor_of = shard_levels(rng, shape, shards, -0.22, 0.18) if shards else 1.0
    values = jax.random.normal(rng, shape, jnp.float32) * width * factor_of
    return jnp.minimum(jnp.maximum(values, -most), most).astype(held_as)


def setup_inputs(seed: int = 0) -> dict:
    arg_keys = jax.random.split(jax.random.key(seed), 13)
    query = draw_query(jax.random.fold_in(arg_keys[12], 71), 0)
    keys = draw_keys(jax.random.fold_in(arg_keys[12], 71), 0)
    values = noise(arg_keys[2], (TOKENS, D), 1.0, 6.0, ((0, 16), (1, 16)))
    out_grad = noise(arg_keys[3], (TOKENS, D), 0.04, 0.625, ((0, 16), (1, 16)))
    gate_left = noise(arg_keys[4], (D, R), (D // 16) ** -0.5, 0.375, ((0, 16),))
    up_left = noise(arg_keys[5], (D, R), (D // 16) ** -0.5, 0.375, ((0, 16),))
    gate_right = noise(arg_keys[6], (R, FF), R ** -0.5, 0.25, ((1, 16),))
    up_right = noise(arg_keys[7], (R, FF), R ** -0.5, 0.25, ((1, 16),))
    down_left = noise(arg_keys[8], (FF, R), R ** -0.5, 0.25, ((0, 16),))
    down_right = noise(arg_keys[9], (R, D), D ** -0.5, 0.09375, ((1, 16),))
    block_order = jax.random.permutation(arg_keys[10], BLOCKS).astype(jnp.int32)
    doc_lengths = ragged(arg_keys[11], DOCS, TOKENS, TOKENS // 2, 1).astype(jnp.int32)
    return dict(query=query, keys=keys, values=values, out_grad=out_grad, gate_left=gate_left, up_left=up_left, gate_right=gate_right, up_right=up_right, down_left=down_left, down_right=down_right, block_order=block_order, doc_lengths=doc_lengths)


def row_positions(block_order):
    half = TOK_DEV // 2
    row_ids = jnp.arange(TOKENS, dtype=jnp.int32)
    return (block_order[row_ids // half] * half + row_ids % half).astype(jnp.int32)


def document_of(positions, doc_lengths):
    limits = jnp.cumsum(doc_lengths).astype(jnp.int32)
    return jnp.sum((positions[:, None] >= limits[None, :]).astype(jnp.int32), axis=1)


def head_part(array, number):
    return lax.dynamic_slice_in_dim(array, number * HD, HD, 1)


def masked_scores(query_head, key_head, allowed):
    scores = jnp.dot(query_head, key_head.T, preferred_element_type=jnp.float32) * (HD ** -0.5)
    return jnp.where(allowed, scores, -jnp.inf)


def log_total(scores):
    highest = jnp.max(scores, axis=1, keepdims=True)
    return highest + jnp.log(jnp.sum(jnp.exp(scores - highest), axis=1, keepdims=True))


def merge_heads(stacked):
    return jnp.transpose(stacked, (1, 0, 2)).reshape(TOKENS, D)


def reference(query, keys, values, out_grad, gate_left, up_left, gate_right, up_right, down_left, down_right, block_order, doc_lengths):
    positions = row_positions(block_order)
    documents = document_of(positions, doc_lengths)
    allowed = (positions[None, :] <= positions[:, None]) & (documents[None, :] == documents[:, None])
    head_ids = jnp.arange(HEADS, dtype=jnp.int32)

    def forward_head(number):
        scores = masked_scores(head_part(query, number), head_part(keys, number), allowed)
        weights = jnp.exp(scores - log_total(scores)).astype(jnp.bfloat16)
        return jnp.dot(weights, head_part(values, number), preferred_element_type=jnp.float32).astype(jnp.bfloat16)

    attended = merge_heads(lax.map(forward_head, head_ids))

    gate_low = jnp.dot(attended, gate_left, preferred_element_type=jnp.float32).astype(jnp.bfloat16)
    up_low = jnp.dot(attended, up_left, preferred_element_type=jnp.float32).astype(jnp.bfloat16)
    gate = jnp.dot(gate_low, gate_right, preferred_element_type=jnp.float32)
    upval = jnp.dot(up_low, up_right, preferred_element_type=jnp.float32)
    sigma = jax.nn.sigmoid(gate)
    hidden = (gate * sigma * upval).astype(jnp.bfloat16)
    down_low = jnp.dot(hidden, down_left, preferred_element_type=jnp.float32).astype(jnp.bfloat16)

    grad_down_right = jnp.dot(down_low.T, out_grad, preferred_element_type=jnp.float32)
    grad_down = jnp.dot(out_grad, down_right.T, preferred_element_type=jnp.float32).astype(jnp.bfloat16)
    grad_hidden = jnp.dot(grad_down, down_left.T, preferred_element_type=jnp.float32)
    grad_down_left = jnp.dot(hidden.T, grad_down, preferred_element_type=jnp.float32)
    grad_gate = (grad_hidden * upval * sigma * (1.0 + gate * (1.0 - sigma))).astype(jnp.bfloat16)
    grad_up = (grad_hidden * gate * sigma).astype(jnp.bfloat16)
    grad_gate_right = jnp.dot(gate_low.T, grad_gate, preferred_element_type=jnp.float32)
    grad_up_right = jnp.dot(up_low.T, grad_up, preferred_element_type=jnp.float32)
    grad_gate_low = jnp.dot(grad_gate, gate_right.T, preferred_element_type=jnp.float32).astype(jnp.bfloat16)
    grad_up_low = jnp.dot(grad_up, up_right.T, preferred_element_type=jnp.float32).astype(jnp.bfloat16)
    grad_gate_left = jnp.dot(attended.T, grad_gate_low, preferred_element_type=jnp.float32)
    grad_up_left = jnp.dot(attended.T, grad_up_low, preferred_element_type=jnp.float32)
    grad_attended = (out_grad.astype(jnp.float32)
                     + jnp.dot(grad_gate_low, gate_left.T, preferred_element_type=jnp.float32)
                     + jnp.dot(grad_up_low, up_left.T, preferred_element_type=jnp.float32)).astype(jnp.bfloat16)

    def backward_head(number):
        query_head = head_part(query, number)
        key_head = head_part(keys, number)
        value_head = head_part(values, number)
        outer_grad = head_part(grad_attended, number)
        scores = masked_scores(query_head, key_head, allowed)
        weights = jnp.exp(scores - log_total(scores))
        delta = jnp.sum(outer_grad.astype(jnp.float32) * head_part(attended, number).astype(jnp.float32), axis=1, keepdims=True)
        weight_grad = jnp.dot(outer_grad, value_head.T, preferred_element_type=jnp.float32)
        score_grad = (weights * (weight_grad - delta) * (HD ** -0.5)).astype(jnp.bfloat16)
        query_out = jnp.dot(score_grad, key_head, preferred_element_type=jnp.float32).astype(jnp.bfloat16)
        key_out = jnp.dot(score_grad.T, query_head, preferred_element_type=jnp.float32).astype(jnp.bfloat16)
        value_out = jnp.dot(weights.astype(jnp.bfloat16).T, outer_grad, preferred_element_type=jnp.float32).astype(jnp.bfloat16)
        return query_out, key_out, value_out

    query_parts, key_parts, value_parts = lax.map(backward_head, head_ids)
    return (merge_heads(query_parts), merge_heads(key_parts), merge_heads(value_parts),
            grad_gate_left, grad_up_left, grad_down_left, grad_gate_right, grad_up_right, grad_down_right)
```

```python
import functools
import math

import jax
import jax.numpy as jnp
from jax import lax
from jax.experimental import pallas as pl
from jax.experimental.pallas import tpu as pltpu
from jax.sharding import PartitionSpec as P

HD = 128
HALF = 128
CHUNK = 4
WIDE = CHUNK * HALF
DOC_BLOCKS = 17
CHUNKS = -(-DOC_BLOCKS // CHUNK)
FACTOR = HD ** (-0.5)
FACTOR2 = FACTOR * math.log2(math.e)
LOW = -1e30
STATS = 16
F32 = jnp.float32
BF16 = jnp.bfloat16
VMEM_BYTES = 32 * 1024 * 1024
GROUP = 16

NT = (((1,), (1,)), ((), ()))
NN = (((1,), (0,)), ((), ()))
TN = (((0,), (0,)), ((), ()))


def mm(left, right, dims):
    return lax.dot_general(left, right, dims, preferred_element_type=F32)


def fill_slots(order_ref, inv_ref):
    for slot in range(order_ref.shape[0]):
        inv_ref[order_ref[slot]] = slot


def doc_edges(lens_ref):
    edges, total = [], jnp.int32(0)
    for number in range(lens_ref.shape[0]):
        total = total + lens_ref[number]
        edges.append(total)
    return edges


def start_of(edges, position):
    start = jnp.zeros_like(position)
    for edge in edges:
        start = jnp.where(edge <= position, edge, start)
    return start


def end_of(edges, position):
    end = jnp.zeros_like(position) + edges[-1]
    for edge in reversed(edges):
        end = jnp.where(edge > position, edge, end)
    return end


def own_slot():
    return lax.axis_index("chip") * 2 + lax.axis_index("core")


def slots_of(inv_ref, first):
    return [
        inv_ref[jnp.minimum(first + turn, inv_ref.shape[0] - 1)] for turn in range(CHUNK)
    ]


def rows_of(ref, slots, cols):
    parts = []
    for slot in slots:
        start = pl.multiple_of((slot % 2) * HALF, HALF)
        parts.append(ref[slot // 4, (slot // 2) % 2, pl.ds(start, HALF), cols])
    return jnp.concatenate(parts, axis=0)


def lane_groups(value, op):
    total = value[:, :HALF]
    for turn in range(1, CHUNK):
        total = op(total, value[:, turn * HALF : (turn + 1) * HALF])
    return total


def query_range(order_ref, edges, half):
    block = order_ref[2 * own_slot() + half]
    first = start_of(edges, block * HALF) // HALF
    turns = (block - first + CHUNK) // CHUNK
    rows = block * HALF + lax.broadcasted_iota(jnp.int32, (HALF, 1), 0)
    return first, turns, rows, start_of(edges, rows)


def key_mask(first, rows, starts):
    lanes = first * HALF + lax.broadcasted_iota(jnp.int32, (HALF, WIDE), 1)
    return (lanes <= rows) & (lanes >= starts)


PLACES = ((0, 0), (3, 0), (1, 0), (0, 1), (3, 1), (1, 1), (2, 0), (2, 1))
PACKED = 4
CTX = ("chip", "core")
BLOCKS = len(PLACES) + 2


def fetch(blocks, all_ref, sems):
    chip, core = lax.axis_index("chip"), lax.axis_index("core")
    row, pair = chip // 2, chip % 2
    rows = blocks[0].shape[0]
    others = [
        pack.at[pl.ds(number * rows, rows)]
        for pack in blocks[len(PLACES) :]
        for number in range(PACKED)
    ]
    copies = []
    for sources, side in ((blocks, core), (others, 1 - core)):
        for (up, across), source in zip(PLACES, sources):
            place = ((row + up) % 4) * 2 + (pair + across) % 2
            copies.append(
                pltpu.make_async_copy(source, all_ref.at[place, side], sems.at[len(copies)])
            )
    for copy in copies:
        copy.start()
    return copies


def fetch_pair(mine_ref, other_ref, all_ref, sems, first):
    core = lax.axis_index("core")
    copies = [
        pltpu.make_async_copy(mine_ref, all_ref.at[:, core], sems.at[first]),
        pltpu.make_async_copy(other_ref, all_ref.at[:, 1 - core], sems.at[first + 1]),
    ]
    for copy in copies:
        copy.start()
    return copies


def settle(copies):
    for copy in copies:
        copy.wait()


def pack_kernel(*refs):
    sources, out_ref = refs[:PACKED], refs[PACKED]
    rows = sources[0].shape[0]
    for number, source in enumerate(sources):
        out_ref[number * rows : (number + 1) * rows] = source[...]


def first_kernel(k_ref, v_ref, og_ref, dr_ref, out_ref, part_ref):
    width = k_ref.shape[1]
    part_ref[...] = mm(og_ref[...], dr_ref[...], NT).astype(BF16)
    for number, source in enumerate((k_ref, v_ref)):
        out_ref[:, number * width : (number + 1) * width] = source[...]


def sum_kernel(*refs):
    out_ref = refs[-1]
    rows = out_ref.shape[0] // GROUP
    base = 0
    for held_ref in refs[:-1]:
        cols = slice(base, base + held_ref.shape[1])
        base = base + held_ref.shape[1]
        total = held_ref[:rows].astype(F32)
        for turn in range(1, GROUP):
            total = total + held_ref[turn * rows : (turn + 1) * rows].astype(F32)
        total = total.astype(BF16)
        for turn in range(GROUP):
            out_ref[turn * rows : (turn + 1) * rows, cols] = total


def cast_kernel(held_ref, *outs):
    rows = outs[0].shape[0]
    for number, out in enumerate(outs):
        out[...] = held_ref[number * rows : (number + 1) * rows].astype(out.dtype)


def token_sum_kernel(held_ref, *outs):
    rows = outs[0].shape[0]
    for number, out in enumerate(outs):
        mine = slice(number * rows, (number + 1) * rows)
        total = held_ref[0, mine].astype(F32)
        for turn in range(1, GROUP):
            total = total + held_ref[turn, mine].astype(F32)
        out[...] = total


def forward_kernel(
    order_ref, lens_ref, q_ref, gl_ref, ul_ref, *refs
):
    blocks, (att_ref, lse_ref, low_ref, inv_ref, s_ref, kv_ref, sems) = refs[:BLOCKS], refs[BLOCKS:]
    copies = fetch(blocks, kv_ref, sems)
    fill_slots(order_ref, inv_ref)
    edges = doc_edges(lens_ref)
    width = q_ref.shape[1]
    heads = width // HD
    settle(copies)
    for half in range(2):
        first, turns, rows, starts = query_range(order_ref, edges, half)
        mine = pl.ds(half * HALF, HALF)

        def score(turn, highs):
            base = first + turn * CHUNK
            keys = rows_of(kv_ref, slots_of(inv_ref, base), slice(0, width))
            ok = key_mask(base, rows, starts)
            out = []
            for head in range(heads):
                cols = slice(head * HD, (head + 1) * HD)
                part = jnp.where(ok, mm(q_ref[mine, cols], keys[:, cols], NT), LOW)
                s_ref[turn, head] = part
                out.append(jnp.maximum(highs[head], lane_groups(part, jnp.maximum)))
            return tuple(out)

        low = jnp.full((HALF, HALF), LOW, F32)
        highs = lax.fori_loop(0, turns, score, (low,) * heads)
        highs = [jnp.max(item, axis=1, keepdims=True) for item in highs]

        def weigh(turn, carried):
            slots = slots_of(inv_ref, first + turn * CHUNK)
            values = rows_of(kv_ref, slots, slice(width, 2 * width))
            out = []
            for head in range(heads):
                cols = slice(head * HD, (head + 1) * HD)
                total, accum = carried[head]
                part = jnp.exp2((s_ref[turn, head] - highs[head]) * FACTOR2)
                total = total + lane_groups(part, jnp.add)
                accum = accum + mm(part.astype(BF16), values[:, cols], NN)
                out.append((total, accum))
            return tuple(out)

        zero = jnp.zeros((HALF, HALF), F32)
        sums = lax.fori_loop(0, turns, weigh, ((zero, zero),) * heads)
        for head in range(heads):
            total = jnp.sum(sums[head][0], axis=1, keepdims=True)
            att_ref[mine, head * HD : (head + 1) * HD] = (sums[head][1] / total).astype(BF16)
            log_norm = highs[head] * FACTOR2 + jnp.log2(total)
            lse_ref[head, mine, :] = jnp.broadcast_to(log_norm, (HALF, HALF))
    rank = gl_ref.shape[1]
    low_ref[:, :rank] = mm(att_ref[...], gl_ref[...], NN).astype(BF16)
    low_ref[:, rank:] = mm(att_ref[...], ul_ref[...], NN).astype(BF16)


def middle_kernel(
    low_ref, grt_ref, urt_ref, dl_ref, back_ref, hidden_ref, gg_ref, gu_ref, mark_ref, acc_ref
):
    rank = dl_ref.shape[1]
    units = dl_ref.shape[0]
    for base in range(0, units, 256):
        cols = slice(base, min(base + 256, units))
        gate = mm(low_ref[:, :rank], grt_ref[cols, :], NT)
        upval = mm(low_ref[:, rank : 2 * rank], urt_ref[cols, :], NT)
        grad_hidden = mm(low_ref[:, 2 * rank :], dl_ref[cols, :], NT)
        sigma = jax.nn.sigmoid(gate)
        silu = gate * sigma
        hidden = (silu * upval).astype(BF16)
        grad_gate = (grad_hidden * upval * sigma * (1.0 + gate * (1.0 - sigma))).astype(BF16)
        grad_up = (grad_hidden * silu).astype(BF16)
        hidden_ref[:, cols] = hidden
        gg_ref[:, cols] = grad_gate
        gu_ref[:, cols] = grad_up
        terms = (
            mm(grad_gate, grt_ref[cols, :], NN),
            mm(grad_up, urt_ref[cols, :], NN),
            mm(hidden, dl_ref[cols, :], NN),
        )
        for number, term in enumerate(terms):
            there = slice(number * rank, (number + 1) * rank)
            if base:
                term = term + acc_ref[:, there]
            if base + 256 >= units:
                back_ref[:, there] = term.astype(BF16)
                mark_ref[...] = term[: mark_ref.shape[0], : mark_ref.shape[1]].astype(BF16)
            else:
                acc_ref[:, there] = term


def outer_terms(pairs, out_ref):
    pieces, height, _ = out_ref.shape
    rows = height // len(pairs)
    step = 256 // rows
    for number, (left, right) in enumerate(pairs):
        for base in range(0, pieces, step):
            term = mm(left[:, base * rows : (base + step) * rows], right[...], TN).astype(BF16)
            for piece in range(step):
                out_ref[base + piece, number * rows : (number + 1) * rows, :] = term[
                    piece * rows : (piece + 1) * rows
                ]


def right_terms_kernel(low_ref, gg_ref, gu_ref, hidden_ref, out_ref):
    rank = low_ref.shape[1] // 3
    pairs = (
        (low_ref.at[:, :rank], gg_ref),
        (low_ref.at[:, rank : 2 * rank], gu_ref),
        (low_ref.at[:, 2 * rank :], hidden_ref),
    )
    outer_terms(pairs, out_ref)


def left_terms_kernel(back_ref, att_ref, og_ref, out_ref):
    rank = back_ref.shape[1] // 3
    pairs = (
        (back_ref.at[:, :rank], att_ref),
        (back_ref.at[:, rank : 2 * rank], att_ref),
        (back_ref.at[:, 2 * rank :], og_ref),
    )
    outer_terms(pairs, out_ref)


def as_rows(column):
    return jnp.transpose(jnp.broadcast_to(column, (HALF, HALF)))[:1]


def split3(value):
    high = value.astype(BF16).astype(F32)
    rest = value - high
    mid = rest.astype(BF16).astype(F32)
    return high, mid, rest - mid


def outgoing_kernel(low_ref, gl_ref, ul_ref, og_ref, att_ref, lse_ref, out_ref):
    rank = gl_ref.shape[1]
    tokens, width = og_ref.shape
    heads = width // HD
    outer = (
        og_ref[...].astype(F32)
        + mm(low_ref[:, :rank], gl_ref[...], NT)
        + mm(low_ref[:, rank : 2 * rank], ul_ref[...], NT)
    ).astype(BF16)
    for place in range(out_ref.shape[0]):
        out_ref[place, :tokens, :] = outer
    product = outer.astype(F32) * att_ref[...].astype(F32)
    stats = []
    for kind in range(2):
        for half in range(2):
            mine = slice(half * HALF, (half + 1) * HALF)
            pieces = []
            for head in range(heads):
                if kind == 0:
                    column = lse_ref[head, mine, :]
                else:
                    column = jnp.sum(
                        product[mine, head * HD : (head + 1) * HD], axis=1, keepdims=True
                    )
                pieces.append(as_rows(column))
            stats.append(jnp.concatenate(pieces, axis=1))
    block = jnp.concatenate(stats, axis=0)
    parts = split3(block)
    block = jnp.concatenate(list(parts) + [jnp.zeros_like(block)], axis=0).astype(BF16)
    for place in range(out_ref.shape[0]):
        out_ref[place, tokens:, :] = block


def query_grad_kernel(
    order_ref, lens_ref, q_ref, att_ref, lse_ref, out_copies_ref, *refs
):
    blocks, (out_ref, inv_ref, kv_ref, do_ref, sems) = refs[:BLOCKS], refs[BLOCKS:]
    copies = fetch(blocks, kv_ref, sems)
    copies.append(
        pltpu.make_async_copy(
            out_copies_ref.at[0, pl.ds(0, do_ref.shape[0])], do_ref, sems.at[len(copies)]
        )
    )
    copies[-1].start()
    fill_slots(order_ref, inv_ref)
    edges = doc_edges(lens_ref)
    width = q_ref.shape[1]
    heads = width // HD
    settle(copies)
    for half in range(2):
        first, turns, rows, starts = query_range(order_ref, edges, half)
        mine = pl.ds(half * HALF, HALF)
        deltas, norms = [], []
        for head in range(heads):
            cols = slice(head * HD, (head + 1) * HD)
            deltas.append(
                jnp.sum(
                    do_ref[mine, cols].astype(F32) * att_ref[mine, cols].astype(F32),
                    axis=1,
                    keepdims=True,
                )
            )
            norms.append(lse_ref[head, mine, :1])

        def step(turn, carried):
            base = first + turn * CHUNK
            slots = slots_of(inv_ref, base)
            keys = rows_of(kv_ref, slots, slice(0, width))
            values = rows_of(kv_ref, slots, slice(width, 2 * width))
            ok = key_mask(base, rows, starts)
            out = []
            for head in range(heads):
                cols = slice(head * HD, (head + 1) * HD)
                raw = mm(q_ref[mine, cols], keys[:, cols], NT)
                weights = jnp.exp2(jnp.where(ok, raw * FACTOR2 - norms[head], LOW))
                back = mm(do_ref[mine, cols], values[:, cols], NT)
                grads = (weights * (back - deltas[head]) * FACTOR).astype(BF16)
                out.append(carried[head] + mm(grads, keys[:, cols], NN))
            return tuple(out)

        zero = jnp.zeros((HALF, HD), F32)
        sums = lax.fori_loop(0, turns, step, (zero,) * heads)
        for head in range(heads):
            out_ref[mine, head * HD : (head + 1) * HD] = sums[head].astype(BF16)


def key_grad_kernel(
    order_ref, lens_ref, k_ref, v_ref, mine_ref, other_ref, all_q_ref,
    gk_ref, gv_ref, inv_ref, stat_ref, q_ref, do_ref, sems
):
    copies = fetch_pair(mine_ref, other_ref, do_ref, sems, 0)
    copies.append(pltpu.make_async_copy(all_q_ref, q_ref, sems.at[2]))
    copies[-1].start()
    fill_slots(order_ref, inv_ref)
    edges = doc_edges(lens_ref)
    heads = k_ref.shape[1] // HD
    tokens = k_ref.shape[0]
    settle(copies)
    for owner in range(GROUP):
        stats = do_ref[owner // 2, owner % 2, tokens:, :].astype(F32)
        stat_ref[owner] = stats[0:4] + stats[4:8] + stats[8:12]
    for half in range(2):
        block = order_ref[2 * own_slot() + half]
        last = end_of(edges, block * HALF + HALF - 1)
        turns = ((last - 1) // HALF - block + CHUNK) // CHUNK
        rows = block * HALF + lax.broadcasted_iota(jnp.int32, (HALF, 1), 0)
        ends = end_of(edges, rows)
        mine = pl.ds(half * HALF, HALF)

        def step(turn, carried):
            base = block + turn * CHUNK
            slots = slots_of(inv_ref, base)
            queries = rows_of(q_ref, slots, slice(None))
            outers = rows_of(do_ref, slots, slice(None))
            norms, deltas = [], []
            for slot in slots:
                norms.append(stat_ref[slot // 2, pl.ds(slot % 2, 1), :])
                deltas.append(stat_ref[slot // 2, pl.ds(2 + slot % 2, 1), :])
            lanes = base * HALF + lax.broadcasted_iota(jnp.int32, (HALF, WIDE), 1)
            ok = (lanes >= rows) & (lanes < ends)
            out = []
            for head in range(heads):
                cols = slice(head * HD, (head + 1) * HD)
                norm = jnp.concatenate([item[:, cols] for item in norms], axis=1)
                delta = jnp.concatenate([item[:, cols] for item in deltas], axis=1)
                raw = mm(k_ref[mine, cols], queries[:, cols], NT)
                weights = jnp.exp2(jnp.where(ok, raw * FACTOR2 - norm, LOW))
                back = mm(v_ref[mine, cols], outers[:, cols], NT)
                grads = (weights * (back - delta) * FACTOR).astype(BF16)
                key_sum, value_sum = carried[head]
                out.append(
                    (
                        key_sum + mm(grads, queries[:, cols], NN),
                        value_sum + mm(weights.astype(BF16), outers[:, cols], NN),
                    )
                )
            return tuple(out)

        zero = jnp.zeros((HALF, HD), F32)
        sums = lax.fori_loop(0, turns, step, ((zero, zero),) * heads)
        for head in range(heads):
            cols = slice(head * HD, (head + 1) * HD)
            gk_ref[mine, cols] = sums[head][0].astype(BF16)
            gv_ref[mine, cols] = sums[head][1].astype(BF16)


def call(
    kernel, outs, scalars=(), arrays=(), remote=(), scratch=(), flops=0, moved=0, limit=VMEM_BYTES
):
    smem = pl.BlockSpec(memory_space=pltpu.SMEM)
    vmem = pl.BlockSpec(memory_space=pltpu.VMEM)
    anywhere = pl.BlockSpec(memory_space=pl.ANY)
    return pl.pallas_call(
        kernel,
        out_shape=tuple(jax.ShapeDtypeStruct(shape, kind) for shape, kind in outs),
        in_specs=[smem] * len(scalars) + [vmem] * len(arrays) + [anywhere] * len(remote),
        out_specs=tuple([vmem] * len(outs)),
        scratch_shapes=list(scratch),
        compiler_params=pltpu.CompilerParams(vmem_limit_bytes=limit),
        cost_estimate=pl.CostEstimate(flops=flops, bytes_accessed=moved, transcendentals=0),
    )(*scalars, *arrays, *remote)


def exchange(value, axis):
    return lax.all_to_all(value, axis, split_axis=0, concat_axis=0, tiled=True)


def head_sum(*held):
    rows, width = held[0].shape[0], sum(item.shape[1] for item in held)
    (copies,) = call(
        sum_kernel, (((rows, width), BF16),), arrays=held, moved=rows * width * 4
    )
    return copies


def token_total(terms):
    pieces, rows, width = terms.shape
    return call(
        token_sum_kernel,
        (((rows // 3, width), F32),) * 3,
        arrays=(exchange(terms, CTX),),
        moved=pieces * rows * width * 2,
    )


def send(value, up, across, other):
    def target(place):
        row, pair, core = place // 4, (place // 2) % 2, place % 2
        return ((row + up) % 4) * 4 + (pair + across) % 2 * 2 + (core + other) % 2

    return lax.ppermute(value, CTX, [(place, target(place)) for place in range(GROUP)])


def packed(blocks):
    rows, width = blocks[0].shape
    (pack,) = call(
        pack_kernel,
        (((PACKED * rows, width), BF16),),
        arrays=blocks,
        moved=4 * PACKED * rows * width,
    )
    return send(pack, 0, 0, 1)


def gather(own, part):
    held = exchange(part, "head")
    stage = (send(own, 1, 0, 0), send(own, 3, 0, 0), send(own, 0, 1, 0))
    own, below, above, beside = lax.optimization_barrier((own, *stage))
    first = (own, below, above, beside)
    stage = (
        send(below, 0, 1, 0), send(beside, 3, 0, 0), send(below, 1, 0, 0), send(below, 1, 1, 0)
    )
    *second, held = lax.optimization_barrier((*stage, held))
    return [*first, *second, packed(first), packed(second)], held


def after(value, *others):
    return lax.optimization_barrier((value, *others))[0]


def local(
    query,
    keys,
    values,
    out_grad,
    gate_left,
    up_left,
    gate_right,
    up_right,
    down_left,
    down_right,
    block_order,
    doc_lengths,
):
    tokens, width = query.shape
    heads = width // HD
    rank = gate_left.shape[1]
    units = down_left.shape[0]
    chips, cores = lax.axis_size("chip"), lax.axis_size("core")
    count = chips * cores
    everything = count * tokens
    places = (block_order, doc_lengths)
    inverse = pltpu.SMEM(block_order.shape, jnp.int32)
    gate_right_t, up_right_t = gate_right.T, up_right.T

    joined, part = call(
        first_kernel,
        (((tokens, 2 * width), BF16), ((tokens, rank), BF16)),
        arrays=(keys, values, out_grad, down_right),
        flops=2 * tokens * rank * width,
        moved=2 << 20,
        limit=60 * 1024 * 1024,
    )
    blocks, held = gather(joined, part)
    all_queries = lax.all_gather(after(query, blocks[6]), CTX, axis=0, tiled=True).reshape(
        chips, cores, tokens, width
    )

    attended, log_norm, part = call(
        forward_kernel,
        (
            ((tokens, width), BF16),
            ((heads, tokens, HALF), F32),
            ((tokens, 2 * rank), BF16),
        ),
        places,
        (query, gate_left, up_left),
        blocks,
        (
            inverse,
            pltpu.VMEM((CHUNKS, heads, HALF, WIDE), F32),
            pltpu.VMEM((chips, cores, tokens, 2 * width), BF16),
            pltpu.SemaphoreType.DMA((GROUP,)),
        ),
        flops=4 * tokens * everything * width,
        moved=64 << 20,
    )
    low = exchange(head_sum(exchange(part, "head"), held), "head")

    back_part, hidden, grad_gate, grad_up, mark = call(
        middle_kernel,
        (
            ((tokens, 3 * rank), BF16),
            ((tokens, units), BF16),
            ((tokens, units), BF16),
            ((tokens, units), BF16),
            ((16, HALF), BF16),
        ),
        arrays=(low, gate_right_t, up_right_t, down_left),
        scratch=(pltpu.VMEM((tokens, 3 * rank), F32),),
        flops=12 * tokens * rank * units,
        moved=4 << 20,
    )
    mark = lax.ppermute(mark, "core", [(0, 1), (1, 0)])
    copies = head_sum(exchange(back_part, "head"))
    back = exchange(copies, "head")

    (terms,) = call(
        right_terms_kernel,
        (((count, 3 * rank // count, units), BF16),),
        arrays=(low, grad_gate, grad_up, after(hidden, mark)),
        flops=6 * tokens * rank * units,
        moved=4 << 20,
    )
    held = lax.psum_scatter(
        terms.reshape(3 * rank, units), CTX, scatter_dimension=0, tiled=True
    )

    (outgoing,) = call(
        outgoing_kernel,
        (((chips, tokens + STATS, width), BF16),),
        arrays=(back, gate_left, up_left, out_grad, attended, log_norm),
        flops=4 * tokens * rank * width,
        moved=1 << 30,
    )
    mine = exchange(outgoing, "chip")
    (terms,) = call(
        left_terms_kernel,
        (((count, 3 * rank // count, width), BF16),),
        arrays=(back, attended, out_grad),
        flops=6 * tokens * rank * width,
        moved=2 << 20,
    )
    (grad_query,) = call(
        query_grad_kernel,
        (((tokens, width), BF16),),
        places,
        (query, attended, log_norm),
        (outgoing, *blocks),
        (
            inverse,
            pltpu.VMEM((chips, cores, tokens, 2 * width), BF16),
            pltpu.VMEM((tokens, width), BF16),
            pltpu.SemaphoreType.DMA((GROUP + 1,)),
        ),
        flops=6 * tokens * everything * width // 2,
        moved=6 << 20,
    )
    mine, grad_query, terms = lax.optimization_barrier((mine, grad_query, terms))
    other = lax.ppermute(mine, "core", [(0, 1), (1, 0)])
    left_sums = token_total(after(terms, other))
    grad_keys, grad_values = call(
        key_grad_kernel,
        (((tokens, width), BF16), ((tokens, width), BF16)),
        places,
        (keys, values),
        (mine, other, all_queries),
        (
            inverse,
            pltpu.VMEM((count, 4, width), F32),
            pltpu.VMEM((chips, cores, tokens, width), BF16),
            pltpu.VMEM((chips, cores, tokens + STATS, width), BF16),
            pltpu.SemaphoreType.DMA((3,)),
        ),
        flops=8 * tokens * everything * width // 2,
        moved=1 << 30,
    )
    right_sums = call(
        cast_kernel,
        (((rank // count, units), F32),) * 3,
        arrays=(after(held, grad_keys),),
        moved=1 << 19,
    )
    return (
        grad_query,
        grad_keys,
        grad_values,
        left_sums[0].T,
        left_sums[1].T,
        right_sums[2].T,
        right_sums[0],
        right_sums[1],
        left_sums[2],
    )


def solution(mesh):
    count = mesh.shape["ctx"]
    mesh = jax.sharding.Mesh(
        mesh.devices.reshape(count // 2, 2, mesh.shape["head"]), ("chip", "core", "head")
    )
    ctx = CTX
    in_specs = (
        P(ctx, "head"),
        P(ctx, "head"),
        P(ctx, "head"),
        P(ctx, "head"),
        P("head", None),
        P("head", None),
        P(None, "head"),
        P(None, "head"),
        P("head", None),
        P(None, "head"),
        P(),
        P(),
    )
    out_specs = (
        P(ctx, "head"),
        P(ctx, "head"),
        P(ctx, "head"),
        P("head", ctx),
        P("head", ctx),
        P("head", ctx),
        P(ctx, "head"),
        P(ctx, "head"),
        P(ctx, "head"),
    )
    return jax.shard_map(local, mesh=mesh, in_specs=in_specs, out_specs=out_specs, check_vma=False)
```

```python
import functools
import math

import jax
import jax.numpy as jnp
from jax import lax
from jax.experimental import pallas as pl
from jax.experimental.pallas import tpu as pltpu
from jax.sharding import PartitionSpec as P

HD = 128
HALF = 128
CHUNK = 4
WIDE = CHUNK * HALF
DOC_BLOCKS = 17
CHUNKS = -(-DOC_BLOCKS // CHUNK)
FACTOR = HD ** (-0.5)
FACTOR2 = FACTOR * math.log2(math.e)
LOW = -1e30
STATS = 16
F32 = jnp.float32
BF16 = jnp.bfloat16
VMEM_BYTES = 32 * 1024 * 1024
GROUP = 16

NT = (((1,), (1,)), ((), ()))
NN = (((1,), (0,)), ((), ()))
TN = (((0,), (0,)), ((), ()))


def mm(left, right, dims):
    return lax.dot_general(left, right, dims, preferred_element_type=F32)


def fill_slots(order_ref, inv_ref):
    for slot in range(order_ref.shape[0]):
        inv_ref[order_ref[slot]] = slot


def doc_edges(lens_ref):
    edges, total = [], jnp.int32(0)
    for number in range(lens_ref.shape[0]):
        total = total + lens_ref[number]
        edges.append(total)
    return edges


def start_of(edges, position):
    start = jnp.zeros_like(position)
    for edge in edges:
        start = jnp.where(edge <= position, edge, start)
    return start


def end_of(edges, position):
    end = jnp.zeros_like(position) + edges[-1]
    for edge in reversed(edges):
        end = jnp.where(edge > position, edge, end)
    return end


def own_slot():
    return lax.axis_index("chip") * 2 + lax.axis_index("core")


def slots_of(inv_ref, first):
    return [
        inv_ref[jnp.minimum(first + turn, inv_ref.shape[0] - 1)] for turn in range(CHUNK)
    ]


def rows_of(ref, slots, cols):
    parts = []
    for slot in slots:
        start = pl.multiple_of((slot % 2) * HALF, HALF)
        parts.append(ref[slot // 4, (slot // 2) % 2, pl.ds(start, HALF), cols])
    return jnp.concatenate(parts, axis=0)


def lane_groups(value, op):
    total = value[:, :HALF]
    for turn in range(1, CHUNK):
        total = op(total, value[:, turn * HALF : (turn + 1) * HALF])
    return total


def query_range(order_ref, edges, half):
    block = order_ref[2 * own_slot() + half]
    first = start_of(edges, block * HALF) // HALF
    turns = (block - first + CHUNK) // CHUNK
    rows = block * HALF + lax.broadcasted_iota(jnp.int32, (HALF, 1), 0)
    return first, turns, rows, start_of(edges, rows)


def key_mask(first, rows, starts):
    lanes = first * HALF + lax.broadcasted_iota(jnp.int32, (HALF, WIDE), 1)
    return (lanes <= rows) & (lanes >= starts)


PLACES = ((0, 0), (3, 0), (1, 0), (0, 1), (3, 1), (1, 1), (2, 0), (2, 1))
PACKED = 4
CTX = ("chip", "core")
BLOCKS = len(PLACES) + 2


def fetch(blocks, all_ref, sems):
    chip, core = lax.axis_index("chip"), lax.axis_index("core")
    row, pair = chip // 2, chip % 2
    rows = blocks[0].shape[0]
    others = [
        pack.at[pl.ds(number * rows, rows)]
        for pack in blocks[len(PLACES) :]
        for number in range(PACKED)
    ]
    copies = []
    for sources, side in ((blocks, core), (others, 1 - core)):
        for (up, across), source in zip(PLACES, sources):
            place = ((row + up) % 4) * 2 + (pair + across) % 2
            copies.append(
                pltpu.make_async_copy(source, all_ref.at[place, side], sems.at[len(copies)])
            )
    for copy in copies:
        copy.start()
    return copies


def fetch_pair(mine_ref, other_ref, all_ref, sems, first):
    core = lax.axis_index("core")
    copies = [
        pltpu.make_async_copy(mine_ref, all_ref.at[:, core], sems.at[first]),
        pltpu.make_async_copy(other_ref, all_ref.at[:, 1 - core], sems.at[first + 1]),
    ]
    for copy in copies:
        copy.start()
    return copies


def settle(copies):
    for copy in copies:
        copy.wait()


def pack_kernel(*refs):
    sources, out_ref = refs[:PACKED], refs[PACKED]
    rows = sources[0].shape[0]
    for number, source in enumerate(sources):
        out_ref[number * rows : (number + 1) * rows] = source[...]


def first_kernel(k_ref, v_ref, og_ref, dr_ref, out_ref, part_ref):
    width = k_ref.shape[1]
    part_ref[...] = mm(og_ref[...], dr_ref[...], NT).astype(BF16)
    for number, source in enumerate((k_ref, v_ref)):
        out_ref[:, number * width : (number + 1) * width] = source[...]


def sum_kernel(*refs):
    out_ref = refs[-1]
    rows = out_ref.shape[0] // GROUP
    base = 0
    for held_ref in refs[:-1]:
        cols = slice(base, base + held_ref.shape[1])
        base = base + held_ref.shape[1]
        total = held_ref[:rows].astype(F32)
        for turn in range(1, GROUP):
            total = total + held_ref[turn * rows : (turn + 1) * rows].astype(F32)
        total = total.astype(BF16)
        for turn in range(GROUP):
            out_ref[turn * rows : (turn + 1) * rows, cols] = total


def cast_kernel(held_ref, *outs):
    rows = outs[0].shape[0]
    for number, out in enumerate(outs):
        out[...] = held_ref[number * rows : (number + 1) * rows].astype(out.dtype)


def token_sum_kernel(held_ref, *outs):
    rows = outs[0].shape[0]
    for number, out in enumerate(outs):
        mine = slice(number * rows, (number + 1) * rows)
        total = held_ref[0, mine].astype(F32)
        for turn in range(1, GROUP):
            total = total + held_ref[turn, mine].astype(F32)
        out[...] = total


def forward_kernel(
    order_ref, lens_ref, q_ref, gl_ref, ul_ref, *refs
):
    blocks, (att_ref, lse_ref, low_ref, inv_ref, s_ref, kv_ref, sems) = refs[:BLOCKS], refs[BLOCKS:]
    copies = fetch(blocks, kv_ref, sems)
    fill_slots(order_ref, inv_ref)
    edges = doc_edges(lens_ref)
    width = q_ref.shape[1]
    heads = width // HD
    settle(copies)
    for half in range(2):
        first, turns, rows, starts = query_range(order_ref, edges, half)
        mine = pl.ds(half * HALF, HALF)

        def score(turn, highs):
            base = first + turn * CHUNK
            keys = rows_of(kv_ref, slots_of(inv_ref, base), slice(0, width))
            ok = key_mask(base, rows, starts)
            out = []
            for head in range(heads):
                cols = slice(head * HD, (head + 1) * HD)
                part = jnp.where(ok, mm(q_ref[mine, cols], keys[:, cols], NT), LOW)
                s_ref[turn, head] = part
                out.append(jnp.maximum(highs[head], lane_groups(part, jnp.maximum)))
            return tuple(out)

        low = jnp.full((HALF, HALF), LOW, F32)
        highs = lax.fori_loop(0, turns, score, (low,) * heads)
        highs = [jnp.max(item, axis=1, keepdims=True) for item in highs]

        def weigh(turn, carried):
            slots = slots_of(inv_ref, first + turn * CHUNK)
            values = rows_of(kv_ref, slots, slice(width, 2 * width))
            out = []
            for head in range(heads):
                cols = slice(head * HD, (head + 1) * HD)
                total, accum = carried[head]
                part = jnp.exp2((s_ref[turn, head] - highs[head]) * FACTOR2)
                total = total + lane_groups(part, jnp.add)
                accum = accum + mm(part.astype(BF16), values[:, cols], NN)
                out.append((total, accum))
            return tuple(out)

        zero = jnp.zeros((HALF, HALF), F32)
        sums = lax.fori_loop(0, turns, weigh, ((zero, zero),) * heads)
        for head in range(heads):
            total = jnp.sum(sums[head][0], axis=1, keepdims=True)
            att_ref[mine, head * HD : (head + 1) * HD] = (sums[head][1] / total).astype(BF16)
            log_norm = highs[head] * FACTOR2 + jnp.log2(total)
            lse_ref[head, mine, :] = jnp.broadcast_to(log_norm, (HALF, HALF))
    rank = gl_ref.shape[1]
    low_ref[:, :rank] = mm(att_ref[...], gl_ref[...], NN).astype(BF16)
    low_ref[:, rank:] = mm(att_ref[...], ul_ref[...], NN).astype(BF16)


def middle_kernel(
    low_ref, grt_ref, urt_ref, dl_ref, back_ref, out_ref, hidden_ref, gg_ref, gu_ref, acc_ref
):
    rank = dl_ref.shape[1]
    units = dl_ref.shape[0]
    for base in range(0, units, 256):
        cols = slice(base, min(base + 256, units))
        gate = mm(low_ref[:, :rank], grt_ref[cols, :], NT)
        upval = mm(low_ref[:, rank : 2 * rank], urt_ref[cols, :], NT)
        grad_hidden = mm(low_ref[:, 2 * rank :], dl_ref[cols, :], NT)
        sigma = jax.nn.sigmoid(gate)
        silu = gate * sigma
        hidden = (silu * upval).astype(BF16)
        grad_gate = (grad_hidden * upval * sigma * (1.0 + gate * (1.0 - sigma))).astype(BF16)
        grad_up = (grad_hidden * silu).astype(BF16)
        hidden_ref[:, cols] = hidden
        gg_ref[:, cols] = grad_gate
        gu_ref[:, cols] = grad_up
        terms = (
            mm(grad_gate, grt_ref[cols, :], NN),
            mm(grad_up, urt_ref[cols, :], NN),
            mm(hidden, dl_ref[cols, :], NN),
        )
        for number, term in enumerate(terms):
            there = slice(number * rank, (number + 1) * rank)
            if base:
                term = term + acc_ref[:, there]
            if base + 256 >= units:
                back_ref[:, there] = term.astype(BF16)
            else:
                acc_ref[:, there] = term
    pairs = (
        (low_ref.at[:, :rank], gg_ref),
        (low_ref.at[:, rank : 2 * rank], gu_ref),
        (low_ref.at[:, 2 * rank :], hidden_ref),
    )
    outer_terms(pairs, out_ref)


def outer_terms(pairs, out_ref):
    pieces, height, _ = out_ref.shape
    rows = height // len(pairs)
    step = 256 // rows
    for number, (left, right) in enumerate(pairs):
        for base in range(0, pieces, step):
            term = mm(left[:, base * rows : (base + step) * rows], right[...], TN).astype(BF16)
            for piece in range(step):
                out_ref[base + piece, number * rows : (number + 1) * rows, :] = term[
                    piece * rows : (piece + 1) * rows
                ]


def left_terms_kernel(back_ref, att_ref, og_ref, out_ref):
    rank = back_ref.shape[1] // 3
    pairs = (
        (back_ref.at[:, :rank], att_ref),
        (back_ref.at[:, rank : 2 * rank], att_ref),
        (back_ref.at[:, 2 * rank :], og_ref),
    )
    outer_terms(pairs, out_ref)


def as_rows(column):
    return jnp.transpose(jnp.broadcast_to(column, (HALF, HALF)))[:1]


def split3(value):
    high = value.astype(BF16).astype(F32)
    rest = value - high
    mid = rest.astype(BF16).astype(F32)
    return high, mid, rest - mid


def outgoing_kernel(low_ref, gl_ref, ul_ref, og_ref, att_ref, lse_ref, out_ref):
    rank = gl_ref.shape[1]
    tokens, width = og_ref.shape
    heads = width // HD
    outer = (
        og_ref[...].astype(F32)
        + mm(low_ref[:, :rank], gl_ref[...], NT)
        + mm(low_ref[:, rank : 2 * rank], ul_ref[...], NT)
    ).astype(BF16)
    for place in range(out_ref.shape[0]):
        out_ref[place, :tokens, :] = outer
    product = outer.astype(F32) * att_ref[...].astype(F32)
    stats = []
    for kind in range(2):
        for half in range(2):
            mine = slice(half * HALF, (half + 1) * HALF)
            pieces = []
            for head in range(heads):
                if kind == 0:
                    column = lse_ref[head, mine, :]
                else:
                    column = jnp.sum(
                        product[mine, head * HD : (head + 1) * HD], axis=1, keepdims=True
                    )
                pieces.append(as_rows(column))
            stats.append(jnp.concatenate(pieces, axis=1))
    block = jnp.concatenate(stats, axis=0)
    parts = split3(block)
    block = jnp.concatenate(list(parts) + [jnp.zeros_like(block)], axis=0).astype(BF16)
    for place in range(out_ref.shape[0]):
        out_ref[place, tokens:, :] = block


def query_grad_kernel(
    order_ref, lens_ref, q_ref, att_ref, lse_ref, out_copies_ref, *refs
):
    blocks, (out_ref, inv_ref, kv_ref, do_ref, sems) = refs[:BLOCKS], refs[BLOCKS:]
    copies = fetch(blocks, kv_ref, sems)
    copies.append(
        pltpu.make_async_copy(
            out_copies_ref.at[0, pl.ds(0, do_ref.shape[0])], do_ref, sems.at[len(copies)]
        )
    )
    copies[-1].start()
    fill_slots(order_ref, inv_ref)
    edges = doc_edges(lens_ref)
    width = q_ref.shape[1]
    heads = width // HD
    settle(copies)
    for half in range(2):
        first, turns, rows, starts = query_range(order_ref, edges, half)
        mine = pl.ds(half * HALF, HALF)
        deltas, norms = [], []
        for head in range(heads):
            cols = slice(head * HD, (head + 1) * HD)
            deltas.append(
                jnp.sum(
                    do_ref[mine, cols].astype(F32) * att_ref[mine, cols].astype(F32),
                    axis=1,
                    keepdims=True,
                )
            )
            norms.append(lse_ref[head, mine, :1])

        def step(turn, carried):
            base = first + turn * CHUNK
            slots = slots_of(inv_ref, base)
            keys = rows_of(kv_ref, slots, slice(0, width))
            values = rows_of(kv_ref, slots, slice(width, 2 * width))
            ok = key_mask(base, rows, starts)
            out = []
            for head in range(heads):
                cols = slice(head * HD, (head + 1) * HD)
                raw = mm(q_ref[mine, cols], keys[:, cols], NT)
                weights = jnp.exp2(jnp.where(ok, raw * FACTOR2 - norms[head], LOW))
                back = mm(do_ref[mine, cols], values[:, cols], NT)
                grads = (weights * (back - deltas[head]) * FACTOR).astype(BF16)
                out.append(carried[head] + mm(grads, keys[:, cols], NN))
            return tuple(out)

        zero = jnp.zeros((HALF, HD), F32)
        sums = lax.fori_loop(0, turns, step, (zero,) * heads)
        for head in range(heads):
            out_ref[mine, head * HD : (head + 1) * HD] = sums[head].astype(BF16)


def key_grad_kernel(
    order_ref, lens_ref, k_ref, v_ref, mine_ref, other_ref, all_q_ref,
    gk_ref, gv_ref, inv_ref, stat_ref, q_ref, do_ref, sems
):
    copies = fetch_pair(mine_ref, other_ref, do_ref, sems, 0)
    copies.append(pltpu.make_async_copy(all_q_ref, q_ref, sems.at[2]))
    copies[-1].start()
    fill_slots(order_ref, inv_ref)
    edges = doc_edges(lens_ref)
    heads = k_ref.shape[1] // HD
    tokens = k_ref.shape[0]
    settle(copies)
    for owner in range(GROUP):
        stats = do_ref[owner // 2, owner % 2, tokens:, :].astype(F32)
        stat_ref[owner] = stats[0:4] + stats[4:8] + stats[8:12]
    for half in range(2):
        block = order_ref[2 * own_slot() + half]
        last = end_of(edges, block * HALF + HALF - 1)
        turns = ((last - 1) // HALF - block + CHUNK) // CHUNK
        rows = block * HALF + lax.broadcasted_iota(jnp.int32, (HALF, 1), 0)
        ends = end_of(edges, rows)
        mine = pl.ds(half * HALF, HALF)

        def step(turn, carried):
            base = block + turn * CHUNK
            slots = slots_of(inv_ref, base)
            queries = rows_of(q_ref, slots, slice(None))
            outers = rows_of(do_ref, slots, slice(None))
            norms, deltas = [], []
            for slot in slots:
                norms.append(stat_ref[slot // 2, pl.ds(slot % 2, 1), :])
                deltas.append(stat_ref[slot // 2, pl.ds(2 + slot % 2, 1), :])
            lanes = base * HALF + lax.broadcasted_iota(jnp.int32, (HALF, WIDE), 1)
            ok = (lanes >= rows) & (lanes < ends)
            out = []
            for head in range(heads):
                cols = slice(head * HD, (head + 1) * HD)
                norm = jnp.concatenate([item[:, cols] for item in norms], axis=1)
                delta = jnp.concatenate([item[:, cols] for item in deltas], axis=1)
                raw = mm(k_ref[mine, cols], queries[:, cols], NT)
                weights = jnp.exp2(jnp.where(ok, raw * FACTOR2 - norm, LOW))
                back = mm(v_ref[mine, cols], outers[:, cols], NT)
                grads = (weights * (back - delta) * FACTOR).astype(BF16)
                key_sum, value_sum = carried[head]
                out.append(
                    (
                        key_sum + mm(grads, queries[:, cols], NN),
                        value_sum + mm(weights.astype(BF16), outers[:, cols], NN),
                    )
                )
            return tuple(out)

        zero = jnp.zeros((HALF, HD), F32)
        sums = lax.fori_loop(0, turns, step, ((zero, zero),) * heads)
        for head in range(heads):
            cols = slice(head * HD, (head + 1) * HD)
            gk_ref[mine, cols] = sums[head][0].astype(BF16)
            gv_ref[mine, cols] = sums[head][1].astype(BF16)


def call(
    kernel, outs, scalars=(), arrays=(), remote=(), scratch=(), flops=0, moved=0, limit=VMEM_BYTES
):
    smem = pl.BlockSpec(memory_space=pltpu.SMEM)
    vmem = pl.BlockSpec(memory_space=pltpu.VMEM)
    anywhere = pl.BlockSpec(memory_space=pl.ANY)
    return pl.pallas_call(
        kernel,
        out_shape=tuple(jax.ShapeDtypeStruct(shape, kind) for shape, kind in outs),
        in_specs=[smem] * len(scalars) + [vmem] * len(arrays) + [anywhere] * len(remote),
        out_specs=tuple([vmem] * len(outs)),
        scratch_shapes=list(scratch),
        compiler_params=pltpu.CompilerParams(vmem_limit_bytes=limit),
        cost_estimate=pl.CostEstimate(flops=flops, bytes_accessed=moved, transcendentals=0),
    )(*scalars, *arrays, *remote)


def exchange(value, axis):
    return lax.all_to_all(value, axis, split_axis=0, concat_axis=0, tiled=True)


def head_sum(*held):
    rows, width = held[0].shape[0], sum(item.shape[1] for item in held)
    (copies,) = call(
        sum_kernel, (((rows, width), BF16),), arrays=held, moved=rows * width * 4
    )
    return copies


def token_total(terms):
    pieces, rows, width = terms.shape
    return call(
        token_sum_kernel,
        (((rows // 3, width), F32),) * 3,
        arrays=(exchange(terms, CTX),),
        moved=pieces * rows * width * 2,
    )


def send(value, up, across, other):
    def target(place):
        row, pair, core = place // 4, (place // 2) % 2, place % 2
        return ((row + up) % 4) * 4 + (pair + across) % 2 * 2 + (core + other) % 2

    return lax.ppermute(value, CTX, [(place, target(place)) for place in range(GROUP)])


def packed(blocks):
    rows, width = blocks[0].shape
    (pack,) = call(
        pack_kernel,
        (((PACKED * rows, width), BF16),),
        arrays=blocks,
        moved=4 * PACKED * rows * width,
    )
    return send(pack, 0, 0, 1)


def gather(own, part):
    held = exchange(part, "head")
    stage = (send(own, 1, 0, 0), send(own, 3, 0, 0), send(own, 0, 1, 0))
    own, below, above, beside = lax.optimization_barrier((own, *stage))
    first = (own, below, above, beside)
    stage = (
        send(below, 0, 1, 0), send(beside, 3, 0, 0), send(below, 1, 0, 0), send(below, 1, 1, 0)
    )
    *second, held = lax.optimization_barrier((*stage, held))
    return [*first, *second, packed(first), packed(second)], held


def after(value, *others):
    return lax.optimization_barrier((value, *others))[0]


def local(
    query,
    keys,
    values,
    out_grad,
    gate_left,
    up_left,
    gate_right,
    up_right,
    down_left,
    down_right,
    block_order,
    doc_lengths,
):
    tokens, width = query.shape
    heads = width // HD
    rank = gate_left.shape[1]
    units = down_left.shape[0]
    chips, cores = lax.axis_size("chip"), lax.axis_size("core")
    count = chips * cores
    everything = count * tokens
    places = (block_order, doc_lengths)
    inverse = pltpu.SMEM(block_order.shape, jnp.int32)
    gate_right_t, up_right_t = gate_right.T, up_right.T

    joined, part = call(
        first_kernel,
        (((tokens, 2 * width), BF16), ((tokens, rank), BF16)),
        arrays=(keys, values, out_grad, down_right),
        flops=2 * tokens * rank * width,
        moved=2 << 20,
        limit=60 * 1024 * 1024,
    )
    blocks, held = gather(joined, part)
    all_queries = lax.all_gather(after(query, blocks[6]), CTX, axis=0, tiled=True).reshape(
        chips, cores, tokens, width
    )

    attended, log_norm, part = call(
        forward_kernel,
        (
            ((tokens, width), BF16),
            ((heads, tokens, HALF), F32),
            ((tokens, 2 * rank), BF16),
        ),
        places,
        (query, gate_left, up_left),
        blocks,
        (
            inverse,
            pltpu.VMEM((CHUNKS, heads, HALF, WIDE), F32),
            pltpu.VMEM((chips, cores, tokens, 2 * width), BF16),
            pltpu.SemaphoreType.DMA((GROUP,)),
        ),
        flops=4 * tokens * everything * width,
        moved=64 << 20,
    )
    low = exchange(head_sum(exchange(part, "head"), held), "head")

    back_part, terms = call(
        middle_kernel,
        (
            ((tokens, 3 * rank), BF16),
            ((count, 3 * rank // count, units), BF16),
        ),
        arrays=(low, gate_right_t, up_right_t, down_left),
        scratch=(
            pltpu.VMEM((tokens, units), BF16),
            pltpu.VMEM((tokens, units), BF16),
            pltpu.VMEM((tokens, units), BF16),
            pltpu.VMEM((tokens, 3 * rank), F32),
        ),
        flops=18 * tokens * rank * units,
        moved=4 << 20,
    )
    held = lax.psum_scatter(
        terms.reshape(3 * rank, units), CTX, scatter_dimension=0, tiled=True
    )
    copies = head_sum(exchange(back_part, "head"))
    back = exchange(copies, "head")

    (outgoing,) = call(
        outgoing_kernel,
        (((chips, tokens + STATS, width), BF16),),
        arrays=(back, gate_left, up_left, out_grad, attended, log_norm),
        flops=4 * tokens * rank * width,
        moved=1 << 30,
    )
    mine = exchange(outgoing, "chip")
    (terms,) = call(
        left_terms_kernel,
        (((count, 3 * rank // count, width), BF16),),
        arrays=(back, attended, out_grad),
        flops=6 * tokens * rank * width,
        moved=2 << 20,
    )
    (grad_query,) = call(
        query_grad_kernel,
        (((tokens, width), BF16),),
        places,
        (query, attended, log_norm),
        (outgoing, *blocks),
        (
            inverse,
            pltpu.VMEM((chips, cores, tokens, 2 * width), BF16),
            pltpu.VMEM((tokens, width), BF16),
            pltpu.SemaphoreType.DMA((GROUP + 1,)),
        ),
        flops=6 * tokens * everything * width // 2,
        moved=6 << 20,
    )
    mine, grad_query, terms = lax.optimization_barrier((mine, grad_query, terms))
    other = lax.ppermute(mine, "core", [(0, 1), (1, 0)])
    left_sums = token_total(after(terms, other))
    grad_keys, grad_values = call(
        key_grad_kernel,
        (((tokens, width), BF16), ((tokens, width), BF16)),
        places,
        (keys, values),
        (mine, other, all_queries),
        (
            inverse,
            pltpu.VMEM((count, 4, width), F32),
            pltpu.VMEM((chips, cores, tokens, width), BF16),
            pltpu.VMEM((chips, cores, tokens + STATS, width), BF16),
            pltpu.SemaphoreType.DMA((3,)),
        ),
        flops=8 * tokens * everything * width // 2,
        moved=1 << 30,
    )
    right_sums = call(
        cast_kernel,
        (((rank // count, units), F32),) * 3,
        arrays=(after(held, grad_keys),),
        moved=1 << 19,
    )
    return (
        grad_query,
        grad_keys,
        grad_values,
        left_sums[0].T,
        left_sums[1].T,
        right_sums[2].T,
        right_sums[0],
        right_sums[1],
        left_sums[2],
    )


def solution(mesh):
    count = mesh.shape["ctx"]
    mesh = jax.sharding.Mesh(
        mesh.devices.reshape(count // 2, 2, mesh.shape["head"]), ("chip", "core", "head")
    )
    ctx = CTX
    in_specs = (
        P(ctx, "head"),
        P(ctx, "head"),
        P(ctx, "head"),
        P(ctx, "head"),
        P("head", None),
        P("head", None),
        P(None, "head"),
        P(None, "head"),
        P("head", None),
        P(None, "head"),
        P(),
        P(),
    )
    out_specs = (
        P(ctx, "head"),
        P(ctx, "head"),
        P(ctx, "head"),
        P("head", ctx),
        P("head", ctx),
        P("head", ctx),
        P(ctx, "head"),
        P(ctx, "head"),
        P(ctx, "head"),
    )
    return jax.shard_map(local, mesh=mesh, in_specs=in_specs, out_specs=out_specs, check_vma=False)
```
